32 devices in a mesh: planes: 8 (over y, x, core), rows: 4 (over z).
Axes of the slice: x: 2, y: 2, z: 4, core: 2. Of those that a mesh axis runs over, the one named last changes fastest.
Arguments:
- observed: float32 [8, 1024, 1024], P('planes', 'rows'), may hold values from -6 to 6
- estimate: float32 [8, 1024, 1024], P('planes', 'rows'), may hold values from -6 to 6
- spectrum: float32 [8, 1024, 1024], P('planes', 'rows'), may hold values from 0.1 to 1
Outputs:
- restored: float32 [8, 1024, 1024], P('planes', 'rows')
- residual: float32 [8, 1024, 1024], P('planes', 'rows')
The draws below stay inside these ranges and needn't reach their ends.
All inputs are finite; a program needn't handle non-finite values.
Results may differ from the reference program's by a relative error of at most 0.00014.
Values sent between devices are 32-bit elements; how exact they have to be, the bound alone decides.
A program may use at most 128 MiB of HBM per device.

```python
import math
import jax
import jax.numpy as jnp
from jax import lax

N = 1024
SWEEPS = 1
ITERS = 1
PLANES = 8


def level_of(rng, shape, split, smallest, top_value):
    gain, own = 1.0, jax.random.fold_in(rng, 6)
    for dim, parts in split:
        draws = jnp.exp(jax.random.uniform(jax.random.fold_in(own, dim), (parts,), jnp.float32, smallest / len(split), top_value / len(split)))
        gain = gain * jnp.repeat(draws, shape[dim] // parts).reshape([-1 if axis == dim else 1 for axis in range(len(shape))])
    return gain


def noise(rng, shape, spread, most, cuts=(), kind=jnp.bfloat16):
    factor_of = level_of(rng, shape, cuts, -0.22, 0.18) if cuts else 1.0
    values = jax.random.normal(rng, shape, jnp.float32) * spread * factor_of
    return jnp.minimum(jnp.maximum(values, -most), most).astype(kind)


def setup_inputs(seed: int = 0) -> dict:
    keys = jax.random.split(jax.random.key(seed), 4)
    observed = noise(keys[0], (PLANES, N, N), 1.0, 6.0, ((0, 8), (1, 4)), jnp.float32)
    estimate = noise(keys[1], (PLANES, N, N), 1.0, 6.0, ((0, 8), (1, 4)), jnp.float32)
    spectrum = jnp.clip(jnp.exp(math.log(1.0) - 2.3025851 * jax.random.uniform(keys[2], (PLANES, N, N), jnp.float32) ** level_of(keys[2], (PLANES, N, N), ((0, 8), (1, 4)), -0.2, 0.2)), 0.1, 1.0)
    return dict(observed=observed, estimate=estimate, spectrum=spectrum)


HUBER_EDGE = 0.5
SMOOTHING = 0.3
PRECISE = lax.Precision.HIGHEST

def cosine_block(freq_start, freq_length, sample_start, sample_length, extent):
    frequency = freq_start + lax.iota(jnp.int32, freq_length)[:, None]
    sample = sample_start + lax.iota(jnp.int32, sample_length)[None, :]
    residue = (2 * sample + 1) * frequency % (4 * extent)
    angles = residue.astype(jnp.float32) * (math.pi / (2.0 * extent))
    norming = jnp.where(frequency == 0, math.sqrt(1.0 / extent), math.sqrt(2.0 / extent)).astype(jnp.float32)
    return jnp.cos(angles) * norming

def forward(source, cosines):
    spectral = jnp.einsum('kj,pjl->pkl', cosines, source, precision=PRECISE)
    return jnp.einsum('pkj,lj->pkl', spectral, cosines, precision=PRECISE)

def inverse(spectral, cosines):
    row_pass = jnp.einsum('kj,pkl->pjl', cosines, spectral, precision=PRECISE)
    return jnp.einsum('pjl,lm->pjm', row_pass, cosines, precision=PRECISE)

def forward_diff(source, dimension):
    extent = source.shape[dimension]
    ahead = lax.slice_in_dim(source, 1, extent, axis=dimension) - lax.slice_in_dim(source, 0, extent - 1, axis=dimension)
    return jnp.concatenate([ahead, jnp.zeros_like(lax.slice_in_dim(source, 0, 1, axis=dimension))], axis=dimension)

def adjoint_diff(flux, dimension):
    extent = flux.shape[dimension]
    earlier = jnp.concatenate([jnp.zeros_like(lax.slice_in_dim(flux, 0, 1, axis=dimension)), lax.slice_in_dim(flux, 0, extent - 1, axis=dimension)], axis=dimension)
    return earlier - flux

def regular(source, weights):
    divergence = jnp.zeros_like(source)
    for dimension in range(3):
        divergence = divergence + adjoint_diff(weights * forward_diff(source, dimension), dimension)
    return SMOOTHING * divergence

def reference(observed, estimate, spectrum):
    side_cells = observed.shape[1]
    cosines = cosine_block(0, side_cells, 0, side_cells, side_cells)
    observed_spectral = spectrum * forward(observed, cosines)
    squared = spectrum * spectrum
    current = estimate
    residual = observed
    for outer_step in range(SWEEPS):
        magnitude = jnp.zeros_like(current)
        for dimension in range(3):
            slope = forward_diff(current, dimension)
            magnitude = magnitude + slope * slope
        weights = 1.0 / jnp.maximum(jnp.sqrt(magnitude), HUBER_EDGE)
        residual = inverse(observed_spectral - squared * forward(current, cosines), cosines) - regular(current, weights)
        direction = residual
        norm_now = jnp.sum(residual * residual)
        for inner_step in range(ITERS):
            image = inverse(squared * forward(direction, cosines), cosines) + regular(direction, weights)
            step_len = norm_now / jnp.sum(direction * image)
            current = current + step_len * direction
            residual = residual - step_len * image
            norm_next = jnp.sum(residual * residual)
            direction = residual + norm_next / norm_now * direction
            norm_now = norm_next
    return (current, residual)
```

```python
import math

import jax
import jax.numpy as jnp
import numpy as np
from jax import lax
from jax.sharding import PartitionSpec as P

HUBER_EDGE = 0.5
SMOOTHING = 0.3


def padded_2(cells, sides, width):
    for axis, dim in sides:
        count = lax.axis_size(axis)
        ends = count - 1
        head = lax.slice_in_dim(cells, 0, width, axis=dim)
        tail = lax.slice_in_dim(cells, cells.shape[dim] - width, cells.shape[dim], axis=dim)
        cells = jnp.concatenate(
            [
                lax.ppermute(tail, axis, [(i, (i + 1) % count) for i in range(ends)]),
                cells,
                lax.ppermute(head, axis, [((i + 1) % count, i) for i in range(ends)]),
            ],
            axis=dim,
        )
    return cells


def cosine_parts(extent):
    frequency = np.arange(extent)[:, None]
    sample = np.arange(extent)[None, :]
    angles = ((2 * sample + 1) * frequency % (4 * extent)) * (math.pi / (2.0 * extent))
    norming = np.where(frequency == 0, math.sqrt(1.0 / extent), math.sqrt(2.0 / extent))
    whole = (np.cos(angles) * norming).astype(np.float32)
    high = whole.astype(jnp.bfloat16)
    low = (whole - high.astype(np.float32)).astype(jnp.bfloat16)
    return high, low


def split_stack(source, axis):
    high = lax.reduce_precision(source, 8, 7)
    low = (source - high).astype(jnp.bfloat16)
    high = high.astype(jnp.bfloat16)
    return jnp.concatenate([high, high, low], axis=axis)


def valid_mask(start_at, length, extent):
    position = start_at + lax.iota(jnp.int32, length)
    return jnp.where((position >= 0) & (position <= extent - 2), 1.0, 0.0).astype(jnp.float32)


def column_diff(source):
    return jnp.concatenate(
        [source[..., 1:] - source[..., :-1], jnp.zeros_like(source[..., :1])], axis=-1
    )


def shards(observed, estimate, spectrum):
    plane_count, row_count, side_cells = observed.shape
    planes, rows = lax.axis_size("planes"), lax.axis_size("rows")
    total_planes = plane_count * planes
    plane_start = lax.axis_index("planes") * plane_count
    row_start = lax.axis_index("rows") * row_count
    high, low = cosine_parts(side_cells)
    over_samples = jnp.asarray(np.concatenate([high, low, high], axis=1))
    over_freqs = jnp.asarray(np.concatenate([high, low, high], axis=0))
    plane_ok = valid_mask(plane_start - 1, plane_count + 1, total_planes)[:, None, None]
    row_ok = valid_mask(row_start - 1, row_count + 1, side_cells)[None, :, None]

    def relay(source):
        return lax.all_to_all(source, "rows", split_axis=2, concat_axis=1, tiled=True)

    def column_forward(source):
        return jnp.einsum(
            "prj,lj->prl", split_stack(source, 2), over_samples, preferred_element_type=jnp.float32
        )

    def row_forward(source):
        return jnp.einsum(
            "kj,pjl->pkl", over_samples, split_stack(source, 1), preferred_element_type=jnp.float32
        )

    def row_inverse(spectral):
        row_pass = jnp.einsum(
            "kj,pkl->pjl", over_freqs, split_stack(spectral, 1), preferred_element_type=jnp.float32
        )
        return lax.all_to_all(row_pass, "rows", split_axis=1, concat_axis=2, tiled=True)

    def column_inverse(source):
        return jnp.einsum(
            "prl,lm->prm", split_stack(source, 2), over_freqs, preferred_element_type=jnp.float32
        )

    def regular(source, weights):
        padded = padded_2(source, (("planes", 0), ("rows", 1)), 1)
        centre = padded[1:-1, 1:-1]
        flux_plane = weights[:, 1:] * plane_ok * (padded[1:, 1:-1] - padded[:-1, 1:-1])
        flux_row = weights[1:, :] * row_ok * (padded[1:-1, 1:] - padded[1:-1, :-1])
        flux_col = weights[1:, 1:] * column_diff(centre)
        lagged_col = jnp.concatenate(
            [jnp.zeros_like(flux_col[..., :1]), flux_col[..., :-1]], axis=-1
        )
        divergence = (
            flux_plane[:-1]
            - flux_plane[1:]
            + (flux_row[:, :-1] - flux_row[:, 1:])
            + (lagged_col - flux_col)
        )
        return SMOOTHING * divergence

    current = estimate
    gain = relay(spectrum)
    seen = relay(column_forward(observed))
    guess = relay(column_forward(current))
    padded = padded_2(current, (("planes", 0), ("rows", 1)), 1)
    corner = padded[: plane_count + 1, : row_count + 1]
    grad_plane = (padded[1:, : row_count + 1] - corner) * plane_ok
    grad_row = (padded[: plane_count + 1, 1:] - corner) * row_ok
    grad_col = column_diff(corner)
    magnitude = jnp.sqrt(grad_plane * grad_plane + grad_row * grad_row + grad_col * grad_col)
    weights = 1.0 / jnp.maximum(magnitude, HUBER_EDGE)
    smooth = regular(current, weights)
    rough = relay(column_forward(smooth))

    blurred = gain * (row_forward(seen) - gain * row_forward(guess))
    filtered = gain * gain * (blurred - row_forward(rough))
    residual = column_inverse(row_inverse(blurred)) - smooth
    image = column_inverse(row_inverse(filtered)) + regular(residual, weights)
    sums = jnp.stack([jnp.sum(residual * residual), jnp.sum(residual * image)])
    everyone = planes * rows
    shared = lax.all_to_all(
        jnp.broadcast_to(sums[None, :, None], (everyone, 2, 128)),
        ("planes", "rows"),
        split_axis=0,
        concat_axis=0,
        tiled=True,
    )
    sums = jnp.sum(shared[:, :, 0], axis=0)
    step_len = sums[0] / sums[1]
    return (current + step_len * residual, residual - step_len * image)


def solution(mesh):
    return jax.shard_map(
        shards,
        mesh=mesh,
        in_specs=(P("planes", "rows", None), P("planes", "rows", None), P("planes", "rows", None)),
        out_specs=(P("planes", "rows", None), P("planes", "rows", None)),
        check_vma=False,
    )
```

```python
import functools
import math

import jax
import jax.numpy as jnp
import numpy as np
from jax import lax
from jax.experimental import pallas as pl
from jax.experimental.pallas import tpu as pltpu
from jax.sharding import PartitionSpec as P

HUBER_EDGE = 0.5
SMOOTHING = 0.3
MESH = pl.DeviceIdType.MESH
F32 = jnp.float32
BF16 = jnp.bfloat16
STRIP = 8
VMEM_LIMIT = 56 * 1024 * 1024


def cosine_parts(extent):
    frequency = np.arange(extent)[:, None]
    sample = np.arange(extent)[None, :]
    angles = ((2 * sample + 1) * frequency % (4 * extent)) * (math.pi / (2.0 * extent))
    norming = np.where(frequency == 0, math.sqrt(1.0 / extent), math.sqrt(2.0 / extent))
    whole = (np.cos(angles) * norming).astype(np.float32)
    high = whole.astype(jnp.bfloat16)
    low = (whole - high.astype(np.float32)).astype(jnp.bfloat16)
    return high, low


def halves(x):
    high = x.astype(BF16)
    return high, (x - high.astype(F32)).astype(BF16)


def product(ah, al, bh, bl):
    dot = functools.partial(jnp.dot, preferred_element_type=F32)
    return dot(ah, bh) + (dot(ah, bl) + dot(al, bh))


def folded(x):
    return jnp.sum(x.reshape(x.shape[0] // 8, 8, x.shape[1]), axis=0)


def kernel(
    planes, rows,
    obs, est, spec, c_hi, c_lo, t_hi, t_lo,
    d_out, image, step_out,
    v, pp, pm, w, w_pm, smooth, d, d_pp, d_pm,
    sent, got, back_sent, back_got, seen, xh, xl, yh, yl,
    acc_rr, acc_dot, part, total, red_rows, red_planes,
    send_sem, recv_sem, halo_send, halo_recv, sum_send, sum_recv, sum2_send, sum2_recv,
):
    p, z = lax.axis_index("planes"), lax.axis_index("rows")
    R, N = est.shape
    L = N // rows
    tile = min(256, N)
    my_row = pl.multiple_of(z * R, R)
    my_col = pl.multiple_of(z * L, L)
    has_pm, has_pp = p > 0, p < planes - 1
    has_up, has_dn = z > 0, z < rows - 1

    v[pl.ds(8, R), :] = est[...]

    barrier = pltpu.get_barrier_semaphore()

    def greet(cond, where):
        @pl.when(cond)
        def _():
            pl.semaphore_signal(barrier, inc=1, device_id=where, device_id_type=MESH)

    for o in range(1, rows):
        pl.semaphore_signal(
            barrier, inc=1, device_id=(p, lax.rem(z + o, rows)), device_id_type=MESH
        )
    for o in range(1, planes):
        pl.semaphore_signal(
            barrier, inc=1, device_id=(lax.rem(p + o, planes), z), device_id_type=MESH
        )
    diagonals = (
        (jnp.logical_and(has_pm, has_dn), (p - 1, z + 1)),
        (jnp.logical_and(has_pp, has_up), (p + 1, z - 1)),
    )
    for cond, where in diagonals:
        greet(cond, where)
    peers = rows - 1 + planes - 1
    for cond, _ in diagonals:
        peers = peers + jnp.where(cond, 1, 0)
    pl.semaphore_wait(barrier, peers)

    def forward_copy(kind, o):
        to = lax.rem(z + o, rows)
        src = spec if kind == 0 else sent.at[kind - 1]
        return pltpu.make_async_remote_copy(
            src_ref=src.at[:, pl.ds(pl.multiple_of(to * L, L), L)],
            dst_ref=got.at[kind, pl.ds(my_row, R), :],
            send_sem=send_sem.at[kind, o],
            recv_sem=recv_sem.at[kind, o],
            device_id=(p, to),
            device_id_type=MESH,
        )

    def back_copy(kind, o):
        to = lax.rem(z + o, rows)
        return pltpu.make_async_remote_copy(
            src_ref=back_sent.at[kind, pl.ds(pl.multiple_of(to * R, R), R), :],
            dst_ref=back_got.at[kind, :, pl.ds(my_col, L)],
            send_sem=send_sem.at[kind + 4, o],
            recv_sem=recv_sem.at[kind + 4, o],
            device_id=(p, to),
            device_id_type=MESH,
        )

    first, last = pl.ds(0, 8), pl.ds(R - 8, 8)
    body = pl.ds(8, R)
    both = jnp.logical_and
    links = [
        (est, pm.at[body, :], (p + 1, z), has_pp, has_pm),
        (est, pp.at[body, :], (p - 1, z), has_pm, has_pp),
        (est.at[last, :], v.at[pl.ds(0, 8), :], (p, z + 1), has_dn, has_up),
        (est.at[first, :], v.at[pl.ds(R + 8, 8), :], (p, z - 1), has_up, has_dn),
        (est.at[last, :], pp.at[pl.ds(0, 8), :], (p - 1, z + 1), both(has_pm, has_dn), both(has_pp, has_up)),
        (est.at[first, :], pm.at[pl.ds(R + 8, 8), :], (p + 1, z - 1), both(has_pp, has_up), both(has_pm, has_dn)),
        (d.at[body, :], d_pm, (p + 1, z), has_pp, has_pm),
        (d.at[body, :], d_pp, (p - 1, z), has_pm, has_pp),
        (d.at[pl.ds(R, 8), :], d.at[pl.ds(0, 8), :], (p, z + 1), has_dn, has_up),
        (d.at[pl.ds(8, 8), :], d.at[pl.ds(R + 8, 8), :], (p, z - 1), has_up, has_dn),
    ]

    def link(i, act):
        src, dst, where, sends, receives = links[i]
        copy = pltpu.make_async_remote_copy(
            src_ref=src, dst_ref=dst, send_sem=halo_send.at[i], recv_sem=halo_recv.at[i],
            device_id=where, device_id_type=MESH,
        )
        @pl.when(receives if act == "recv" else sends)
        def _():
            if act == "start":
                copy.start()
            elif act == "recv":
                copy.wait_recv()
            else:
                copy.wait_send()

    for i in (2, 3, 4, 5):
        link(i, "start")
    for o in range(1, rows):
        forward_copy(0, o).start()
    for i in (0, 1):
        link(i, "start")
    got[0, pl.ds(my_row, R), :] = spec[:, pl.ds(my_col, L)]

    def columns_forward(kind, source):
        @pl.loop(0, R // 32)
        def _(i):
            strip = pl.ds(pl.multiple_of(i * 32, 32), 32)
            xh[strip, :], xl[strip, :] = halves(source[strip, :])

        @pl.loop(1, rows + 1)
        def _(o):
            at = pl.ds(pl.multiple_of(lax.rem(z + o, rows) * L, L), L)
            sent[kind - 1, :, at] = product(xh[...], xl[...], t_hi[:, at], t_lo[:, at])

            @pl.when(o < rows)
            def _():
                forward_copy(kind, o).start()

        got[kind, pl.ds(my_row, R), :] = sent[kind - 1, :, pl.ds(my_col, L)]

    columns_forward(1, obs)
    columns_forward(2, est)

    column = lax.broadcasted_iota(jnp.int32, (STRIP, N), 1)
    strip_row = lax.broadcasted_iota(jnp.int32, (STRIP, N), 0)
    plane_at = jnp.zeros((STRIP, N), jnp.int32) + p

    def column_slope(x):
        return jnp.where(column < N - 1, pltpu.roll(x, N - 1, 1) - x, 0.0)

    def weight(x, ahead, below, plane_ok, row_at):
        slope_p = jnp.where(plane_ok, ahead - x, 0.0)
        slope_r = jnp.where(jnp.logical_and(row_at >= 0, row_at < N - 1), below - x, 0.0)
        slope_c = column_slope(x)
        size = jnp.sqrt(slope_p * slope_p + slope_r * slope_r + slope_c * slope_c)
        return 1.0 / jnp.maximum(size, HUBER_EDGE)

    for i in range(6):
        link(i, "recv")

    @pl.loop(0, R // STRIP + 1)
    def _(i):
        t = pl.multiple_of(i * STRIP, STRIP)
        block = v[pl.ds(t, STRIP + 8), :]
        w[pl.ds(t, STRIP), :] = weight(
            block[:STRIP], pp[pl.ds(t, STRIP), :], block[1 : STRIP + 1],
            plane_at < planes - 1, my_row + t - 8 + strip_row,
        )

    @pl.loop(0, R // STRIP)
    def _(i):
        t = pl.multiple_of(i * STRIP, STRIP)
        block = pm[pl.ds(t + 8, STRIP + 8), :]
        w_pm[pl.ds(t, STRIP), :] = weight(
            block[:STRIP], est[pl.ds(t, STRIP), :], block[1 : STRIP + 1],
            plane_at > 0, my_row + t + strip_row,
        )

    def regular(x, x_pm, x_pp, shift, out):
        @pl.loop(0, R // STRIP)
        def _(i):
            t = pl.multiple_of(i * STRIP, STRIP)
            block = x[pl.ds(t, STRIP + 16), :]
            here = block[8 : 8 + STRIP]
            weights = w[pl.ds(t, STRIP + 8), :]
            w_here, w_up = weights[8:], weights[7 : 7 + STRIP]
            at = my_row + t + strip_row
            behind = x_pm[pl.ds(t + shift, STRIP), :]
            ahead = x_pp[pl.ds(t + shift, STRIP), :]
            in_r = jnp.where(at > 0, w_up * (here - block[7 : 7 + STRIP]), 0.0)
            out_r = jnp.where(at < N - 1, w_here * (block[9 : 9 + STRIP] - here), 0.0)
            in_p = jnp.where(plane_at > 0, w_pm[pl.ds(t, STRIP), :] * (here - behind), 0.0)
            out_p = jnp.where(plane_at < planes - 1, w_here * (ahead - here), 0.0)
            out_c = w_here * column_slope(here)
            in_c = pltpu.roll(out_c, 1, 1)
            out[pl.ds(t, STRIP), :] = SMOOTHING * (
                (in_p - out_p) + (in_r - out_r) + (in_c - out_c)
            )

    regular(v, pm, pp, 8, smooth)
    columns_forward(3, smooth)

    def arrived(kind):
        @pl.loop(1, rows)
        def _(o):
            forward_copy(kind, o).wait_recv()

    def split_columns(source):
        @pl.loop(0, N // 128)
        def _(i):
            strip = pl.ds(pl.multiple_of(i * 128, 128), 128)
            yh[strip, :], yl[strip, :] = halves(source[strip, :])

    def row_forward(kind, finish):
        split_columns(got.at[kind])

        @pl.loop(0, N // tile)
        def _(i):
            at = pl.ds(pl.multiple_of(i * tile, tile), tile)
            finish(at, product(c_hi[at, :], c_lo[at, :], yh[...], yl[...]))

    def row_inverse(kind, source):
        split_columns(source)

        @pl.loop(1, rows + 1)
        def _(o):
            at = pl.ds(pl.multiple_of(lax.rem(z + o, rows) * R, R), R)
            back_sent[kind, at, :] = product(t_hi[at, :], t_lo[at, :], yh[...], yl[...])

            @pl.when(o < rows)
            def _():
                back_copy(kind, o).start()

        back_got[kind, :, pl.ds(my_col, L)] = back_sent[kind, pl.ds(my_row, R), :]

    def column_inverse(kind, finish):
        @pl.loop(1, rows)
        def _(o):
            back_copy(kind, o).wait_recv()

        @pl.loop(0, R // 32)
        def _(i):
            strip = pl.ds(pl.multiple_of(i * 32, 32), 32)
            xh[strip, :], xl[strip, :] = halves(back_got[kind, strip, :])

        @pl.loop(0, N // tile)
        def _(i):
            at = pl.ds(pl.multiple_of(i * tile, tile), tile)
            finish(at, product(xh[...], xl[...], c_hi[:, at], c_lo[:, at]))

    def keep_seen(at, spectral):
        seen[at, :] = spectral

    def keep_blurred(at, spectral):
        gain = got[0, at, :]
        seen[at, :] = gain * (seen[at, :] - gain * spectral)

    def keep_filtered(at, spectral):
        gain = got[0, at, :]
        seen[at, :] = gain * gain * (seen[at, :] - spectral)

    arrived(0)
    arrived(1)
    row_forward(1, keep_seen)
    arrived(2)
    row_forward(2, keep_blurred)
    row_inverse(0, seen)
    arrived(3)
    row_forward(3, keep_filtered)
    row_inverse(1, seen)

    acc_rr[...] = jnp.zeros_like(acc_rr)
    acc_dot[...] = jnp.zeros_like(acc_dot)

    def keep_residual(at, x):
        x = x - smooth[:, at]
        d[pl.ds(8, R), at] = x
        d_out[:, at] = x
        acc_rr[...] += folded(x * x)

    def keep_image(at, x):
        x = x + image[:, at]
        image[:, at] = x
        acc_dot[...] += folded(x * d_out[:, at])

    column_inverse(0, keep_residual)
    for i in (8, 9, 6, 7):
        link(i, "start")
    for i in (6, 7, 8, 9):
        link(i, "recv")
    regular(d, d_pm, d_pp, 0, image)
    column_inverse(1, keep_image)

    rr, dot = jnp.sum(acc_rr[...]), jnp.sum(acc_dot[...])
    which = lax.broadcasted_iota(jnp.int32, (8, 128), 0)
    part[...] = jnp.where(which == 0, rr, dot)

    def row_sum(o):
        return pltpu.make_async_remote_copy(
            src_ref=part, dst_ref=red_rows.at[o - 1],
            send_sem=sum_send.at[o], recv_sem=sum_recv.at[o],
            device_id=(p, lax.rem(z + o, rows)), device_id_type=MESH,
        )

    def plane_sum(o):
        return pltpu.make_async_remote_copy(
            src_ref=total, dst_ref=red_planes.at[o - 1],
            send_sem=sum2_send.at[o], recv_sem=sum2_recv.at[o],
            device_id=(lax.rem(p + o, planes), z), device_id_type=MESH,
        )

    for o in range(1, rows):
        row_sum(o).start()
    value = part[...]
    for o in range(1, rows):
        row_sum(o).wait_recv()
        value = value + red_rows[o - 1]
    total[...] = value
    for o in range(1, planes):
        plane_sum(o).start()
    for o in range(1, planes):
        plane_sum(o).wait_recv()
        value = value + red_planes[o - 1]
    step_out[...] = jnp.broadcast_to(value[0:1] / value[1:2], (8, 128))

    @pl.loop(1, rows)
    def _(o):
        for kind in range(4):
            forward_copy(kind, o).wait_send()
        for kind in range(2):
            back_copy(kind, o).wait_send()
        row_sum(o).wait_send()

    for o in range(1, planes):
        plane_sum(o).wait_send()
    for i in range(10):
        link(i, "send")


def shards(observed, estimate, spectrum):
    R, N = observed.shape[1:]
    planes, rows = lax.axis_size("planes"), lax.axis_size("rows")
    assert observed.shape[0] == 1
    L = N // rows
    high, low = cosine_parts(N)
    tile = min(256, N)
    vmem = pl.BlockSpec(memory_space=pltpu.VMEM)
    field, padded = pltpu.VMEM((R, N), F32), pltpu.VMEM((R + 16, N), F32)
    tiles = lambda *lead: pltpu.VMEM(lead + (8, 128), F32)
    dma = lambda *shape: pltpu.SemaphoreType.DMA(shape)
    direction, image, step = pl.pallas_call(
        functools.partial(kernel, planes, rows),
        out_shape=(
            jax.ShapeDtypeStruct((R, N), F32),
            jax.ShapeDtypeStruct((R, N), F32),
            jax.ShapeDtypeStruct((8, 128), F32),
        ),
        in_specs=[vmem] * 7,
        out_specs=(vmem,) * 3,
        scratch_shapes=[
            padded, padded, padded, padded, field, field, padded, field, field,
            pltpu.VMEM((3, R, N), F32),
            pltpu.VMEM((4, N, L), F32),
            pltpu.VMEM((2, N, L), F32),
            pltpu.VMEM((2, R, N), F32),
            pltpu.VMEM((N, L), F32),
            pltpu.VMEM((R, N), BF16), pltpu.VMEM((R, N), BF16),
            pltpu.VMEM((N, L), BF16), pltpu.VMEM((N, L), BF16),
            pltpu.VMEM((8, tile), F32), pltpu.VMEM((8, tile), F32),
            tiles(), tiles(), tiles(rows - 1), tiles(planes - 1),
            dma(6, rows), dma(6, rows), dma(10), dma(10),
            dma(rows), dma(rows), dma(planes), dma(planes),
        ],
        compiler_params=pltpu.CompilerParams(
            collective_id=0, has_side_effects=True, vmem_limit_bytes=VMEM_LIMIT
        ),
        name="deconvolve",
    )(
        observed[0], estimate[0], spectrum[0],
        jnp.asarray(high), jnp.asarray(low),
        jnp.asarray(np.ascontiguousarray(high.T)), jnp.asarray(np.ascontiguousarray(low.T)),
    )
    step = step[0, 0]
    return (estimate + step * direction[None], (direction - step * image)[None])


def solution(mesh):
    return jax.shard_map(
        shards,
        mesh=mesh,
        in_specs=(P("planes", "rows", None), P("planes", "rows", None), P("planes", "rows", None)),
        out_specs=(P("planes", "rows", None), P("planes", "rows", None)),
        check_vma=False,
    )
```

```python
import functools
import math

import jax
import jax.numpy as jnp
import numpy as np
from jax import lax
from jax.experimental import pallas as pl
from jax.experimental.pallas import tpu as pltpu
from jax.sharding import PartitionSpec as P

HUBER_EDGE = 0.5
SMOOTHING = 0.3
MESH = pl.DeviceIdType.MESH
F32 = jnp.float32
BF16 = jnp.bfloat16
STRIP = 8
VMEM_LIMIT = 56 * 1024 * 1024


def cosine_parts(extent):
    frequency = np.arange(extent)[:, None]
    sample = np.arange(extent)[None, :]
    angles = ((2 * sample + 1) * frequency % (4 * extent)) * (math.pi / (2.0 * extent))
    norming = np.where(frequency == 0, math.sqrt(1.0 / extent), math.sqrt(2.0 / extent))
    whole = (np.cos(angles) * norming).astype(np.float32)
    high = whole.astype(jnp.bfloat16)
    low = (whole - high.astype(np.float32)).astype(jnp.bfloat16)
    return high, low


def halves(x):
    high = x.astype(BF16)
    return high, (x - high.astype(F32)).astype(BF16)


def product(ah, al, bh, bl):
    dot = functools.partial(jnp.dot, preferred_element_type=F32)
    return dot(ah, bh) + (dot(ah, bl) + dot(al, bh))


def folded(x):
    return jnp.sum(x.reshape(x.shape[0] // 8, 8, x.shape[1]), axis=0)


def kernel(
    planes, rows,
    obs, est, spec, c_hi, c_lo, t_hi, t_lo,
    restored, image,
    v, pp, pm, w, w_pm, smooth, d, d_pp, d_pm,
    sent, got, back_sent, back_got, seen, xh, xl, yh, yl,
    acc_rr, acc_dot, part, total, red_rows, red_planes,
    send_sem, recv_sem, halo_send, halo_recv, sum_send, sum_recv, sum2_send, sum2_recv,
):
    p, z = lax.axis_index("planes"), lax.axis_index("rows")
    R, N = est.shape
    L = N // rows
    tile = min(256, N)
    my_row = pl.multiple_of(z * R, R)
    my_col = pl.multiple_of(z * L, L)
    has_pm, has_pp = p > 0, p < planes - 1
    has_up, has_dn = z > 0, z < rows - 1

    v[pl.ds(8, R), :] = est[...]

    barrier = pltpu.get_barrier_semaphore()

    def greet(cond, where):
        @pl.when(cond)
        def _():
            pl.semaphore_signal(barrier, inc=1, device_id=where, device_id_type=MESH)

    for o in range(1, rows):
        pl.semaphore_signal(
            barrier, inc=1, device_id=(p, lax.rem(z + o, rows)), device_id_type=MESH
        )
    for o in range(1, planes):
        pl.semaphore_signal(
            barrier, inc=1, device_id=(lax.rem(p + o, planes), z), device_id_type=MESH
        )
    diagonals = (
        (jnp.logical_and(has_pm, has_dn), (p - 1, z + 1)),
        (jnp.logical_and(has_pp, has_up), (p + 1, z - 1)),
    )
    for cond, where in diagonals:
        greet(cond, where)
    peers = rows - 1 + planes - 1
    for cond, _ in diagonals:
        peers = peers + jnp.where(cond, 1, 0)
    pl.semaphore_wait(barrier, peers)

    def forward_copy(kind, o):
        to = lax.rem(z + o, rows)
        src = spec if kind == 0 else sent.at[kind - 1]
        return pltpu.make_async_remote_copy(
            src_ref=src.at[:, pl.ds(pl.multiple_of(to * L, L), L)],
            dst_ref=got.at[kind, pl.ds(my_row, R), :],
            send_sem=send_sem.at[kind, o],
            recv_sem=recv_sem.at[kind, o],
            device_id=(p, to),
            device_id_type=MESH,
        )

    half = R // 2

    def back_copy(kind, o, part_at=0):
        to = lax.rem(z + o, rows)
        length = half if kind == 0 else R
        start = pl.multiple_of(to * R + part_at * half, half)
        return pltpu.make_async_remote_copy(
            src_ref=back_sent.at[kind, pl.ds(start, length), :],
            dst_ref=back_got.at[kind, pl.ds(part_at * half, length), pl.ds(my_col, L)],
            send_sem=send_sem.at[4 + 2 * kind + part_at, o],
            recv_sem=recv_sem.at[4 + 2 * kind + part_at, o],
            device_id=(p, to),
            device_id_type=MESH,
        )

    first, last = pl.ds(0, 8), pl.ds(R - 8, 8)
    body = pl.ds(8, R)
    top, low = pl.ds(8, half), pl.ds(8 + half, half)
    both = jnp.logical_and
    links = [
        (est, pm.at[body, :], (p + 1, z), has_pp, has_pm),
        (est, pp.at[body, :], (p - 1, z), has_pm, has_pp),
        (est.at[last, :], v.at[pl.ds(0, 8), :], (p, z + 1), has_dn, has_up),
        (est.at[first, :], v.at[pl.ds(R + 8, 8), :], (p, z - 1), has_up, has_dn),
        (est.at[last, :], pp.at[pl.ds(0, 8), :], (p - 1, z + 1), both(has_pm, has_dn), both(has_pp, has_up)),
        (est.at[first, :], pm.at[pl.ds(R + 8, 8), :], (p + 1, z - 1), both(has_pp, has_up), both(has_pm, has_dn)),
        (d.at[top, :], d_pm.at[pl.ds(0, half), :], (p + 1, z), has_pp, has_pm),
        (d.at[top, :], d_pp.at[pl.ds(0, half), :], (p - 1, z), has_pm, has_pp),
        (d.at[pl.ds(R, 8), :], d.at[pl.ds(0, 8), :], (p, z + 1), has_dn, has_up),
        (d.at[pl.ds(8, 8), :], d.at[pl.ds(R + 8, 8), :], (p, z - 1), has_up, has_dn),
        (d.at[low, :], d_pm.at[pl.ds(half, half), :], (p + 1, z), has_pp, has_pm),
        (d.at[low, :], d_pp.at[pl.ds(half, half), :], (p - 1, z), has_pm, has_pp),
    ]

    def link(i, act):
        src, dst, where, sends, receives = links[i]
        copy = pltpu.make_async_remote_copy(
            src_ref=src, dst_ref=dst, send_sem=halo_send.at[i], recv_sem=halo_recv.at[i],
            device_id=where, device_id_type=MESH,
        )
        @pl.when(receives if act == "recv" else sends)
        def _():
            if act == "start":
                copy.start()
            elif act == "recv":
                copy.wait_recv()
            else:
                copy.wait_send()

    for i in (2, 3, 4, 5):
        link(i, "start")
    for o in range(1, rows):
        forward_copy(0, o).start()
    for i in (0, 1):
        link(i, "start")
    got[0, pl.ds(my_row, R), :] = spec[:, pl.ds(my_col, L)]

    def columns_forward(kind, source):
        @pl.loop(0, R // 32)
        def _(i):
            strip = pl.ds(pl.multiple_of(i * 32, 32), 32)
            xh[strip, :], xl[strip, :] = halves(source[strip, :])

        @pl.loop(1, rows + 1)
        def _(o):
            at = pl.ds(pl.multiple_of(lax.rem(z + o, rows) * L, L), L)
            sent[kind - 1, :, at] = product(xh[...], xl[...], t_hi[:, at], t_lo[:, at])

            if kind != 3:
                @pl.when(o < rows)
                def _():
                    forward_copy(kind, o).start()

        got[kind, pl.ds(my_row, R), :] = sent[kind - 1, :, pl.ds(my_col, L)]

    columns_forward(1, obs)
    columns_forward(2, est)

    column = lax.broadcasted_iota(jnp.int32, (STRIP, N), 1)
    strip_row = lax.broadcasted_iota(jnp.int32, (STRIP, N), 0)
    plane_at = jnp.zeros((STRIP, N), jnp.int32) + p

    def column_slope(x):
        return jnp.where(column < N - 1, pltpu.roll(x, N - 1, 1) - x, 0.0)

    def weight(x, ahead, below, plane_ok, row_at):
        slope_p = jnp.where(plane_ok, ahead - x, 0.0)
        slope_r = jnp.where(jnp.logical_and(row_at >= 0, row_at < N - 1), below - x, 0.0)
        slope_c = column_slope(x)
        size = jnp.sqrt(slope_p * slope_p + slope_r * slope_r + slope_c * slope_c)
        return 1.0 / jnp.maximum(size, HUBER_EDGE)

    for i in range(6):
        link(i, "recv")

    @pl.loop(0, R // STRIP + 1)
    def _(i):
        t = pl.multiple_of(i * STRIP, STRIP)
        block = v[pl.ds(t, STRIP + 8), :]
        w[pl.ds(t, STRIP), :] = weight(
            block[:STRIP], pp[pl.ds(t, STRIP), :], block[1 : STRIP + 1],
            plane_at < planes - 1, my_row + t - 8 + strip_row,
        )

    @pl.loop(0, R // STRIP)
    def _(i):
        t = pl.multiple_of(i * STRIP, STRIP)
        block = pm[pl.ds(t + 8, STRIP + 8), :]
        w_pm[pl.ds(t, STRIP), :] = weight(
            block[:STRIP], est[pl.ds(t, STRIP), :], block[1 : STRIP + 1],
            plane_at > 0, my_row + t + strip_row,
        )

    def regular(x, x_pm, x_pp, shift, out, begin=0, end=R):
        @pl.loop(begin // STRIP, end // STRIP)
        def _(i):
            t = pl.multiple_of(i * STRIP, STRIP)
            block = x[pl.ds(t, STRIP + 16), :]
            here = block[8 : 8 + STRIP]
            weights = w[pl.ds(t, STRIP + 8), :]
            w_here, w_up = weights[8:], weights[7 : 7 + STRIP]
            at = my_row + t + strip_row
            behind = x_pm[pl.ds(t + shift, STRIP), :]
            ahead = x_pp[pl.ds(t + shift, STRIP), :]
            in_r = jnp.where(at > 0, w_up * (here - block[7 : 7 + STRIP]), 0.0)
            out_r = jnp.where(at < N - 1, w_here * (block[9 : 9 + STRIP] - here), 0.0)
            in_p = jnp.where(plane_at > 0, w_pm[pl.ds(t, STRIP), :] * (here - behind), 0.0)
            out_p = jnp.where(plane_at < planes - 1, w_here * (ahead - here), 0.0)
            out_c = w_here * column_slope(here)
            in_c = pltpu.roll(out_c, 1, 1)
            out[pl.ds(t, STRIP), :] = SMOOTHING * (
                (in_p - out_p) + (in_r - out_r) + (in_c - out_c)
            )

    regular(v, pm, pp, 8, smooth)
    columns_forward(3, smooth)

    @pl.loop(1, rows)
    def _(o):
        forward_copy(2, o).wait_send()
        forward_copy(3, o).start()

    def arrived(kind):
        @pl.loop(1, rows)
        def _(o):
            forward_copy(kind, o).wait_recv()

    def split_columns(source):
        @pl.loop(0, N // 128)
        def _(i):
            strip = pl.ds(pl.multiple_of(i * 128, 128), 128)
            yh[strip, :], yl[strip, :] = halves(source[strip, :])

    def row_forward(kind, finish):
        split_columns(got.at[kind])

        @pl.loop(0, N // tile)
        def _(i):
            at = pl.ds(pl.multiple_of(i * tile, tile), tile)
            finish(at, product(c_hi[at, :], c_lo[at, :], yh[...], yl[...]))

    def row_inverse(kind, source):
        split_columns(source)
        length = half if kind == 0 else R
        for part_at in range(R // length):
            @pl.loop(1, rows + 1)
            def _(o):
                to = lax.rem(z + o, rows)
                at = pl.ds(pl.multiple_of(to * R + part_at * half, half), length)
                back_sent[kind, at, :] = product(t_hi[at, :], t_lo[at, :], yh[...], yl[...])

                if kind == 0:
                    @pl.when(o < rows)
                    def _():
                        back_copy(kind, o, part_at).start()

        back_got[kind, :, pl.ds(my_col, L)] = back_sent[kind, pl.ds(my_row, R), :]

    def column_inverse(kind, part_at, finish):
        @pl.loop(1, rows)
        def _(o):
            back_copy(kind, o, part_at).wait_recv()

        length = half if kind == 0 else R
        here = pl.ds(part_at * half, length)

        @pl.loop(0, length // 16)
        def _(i):
            strip = pl.ds(pl.multiple_of(part_at * half + i * 16, 16), 16)
            xh[strip, :], xl[strip, :] = halves(back_got[kind, strip, :])

        @pl.loop(0, N // tile)
        def _(i):
            at = pl.ds(pl.multiple_of(i * tile, tile), tile)
            finish(at, product(xh[here, :], xl[here, :], c_hi[:, at], c_lo[:, at]))

    def keep_seen(at, spectral):
        seen[at, :] = spectral

    def keep_blurred(at, spectral):
        gain = got[0, at, :]
        seen[at, :] = gain * (seen[at, :] - gain * spectral)

    def keep_filtered(at, spectral):
        gain = got[0, at, :]
        seen[at, :] = gain * gain * (seen[at, :] - spectral)

    arrived(0)
    arrived(1)
    row_forward(1, keep_seen)
    arrived(2)
    row_forward(2, keep_blurred)
    row_inverse(0, seen)
    arrived(3)
    row_forward(3, keep_filtered)
    row_inverse(1, seen)

    acc_rr[...] = jnp.zeros_like(acc_rr)
    acc_dot[...] = jnp.zeros_like(acc_dot)

    def keep_residual(part_at, at, x):
        here = pl.ds(part_at * half, half)
        x = x - smooth[here, at]
        d[pl.ds(8 + part_at * half, half), at] = x
        acc_rr[...] += folded(x * x)

    def keep_image(at, x):
        x = x + image[:, at]
        image[:, at] = x
        acc_dot[...] += folded(x * d[pl.ds(8, R), at])

    column_inverse(0, 0, functools.partial(keep_residual, 0))
    for i in (9, 6, 7):
        link(i, "start")

    @pl.loop(1, rows)
    def _(o):
        back_copy(0, o, 0).wait_send()
        back_copy(0, o, 1).wait_send()
        back_copy(1, o).start()

    column_inverse(0, 1, functools.partial(keep_residual, 1))
    for i in (8, 10, 11):
        link(i, "start")
    for i in (6, 7, 8):
        link(i, "recv")
    regular(d, d_pm, d_pp, 0, image, 0, half)
    for i in (9, 10, 11):
        link(i, "recv")
    regular(d, d_pm, d_pp, 0, image, half, R)
    column_inverse(1, 0, keep_image)

    rr, dot = jnp.sum(acc_rr[...]), jnp.sum(acc_dot[...])
    which = lax.broadcasted_iota(jnp.int32, (8, 128), 0)
    part[...] = jnp.where(which == 0, rr, dot)

    def row_sum(o):
        return pltpu.make_async_remote_copy(
            src_ref=part, dst_ref=red_rows.at[o - 1],
            send_sem=sum_send.at[o], recv_sem=sum_recv.at[o],
            device_id=(p, lax.rem(z + o, rows)), device_id_type=MESH,
        )

    def plane_sum(o):
        return pltpu.make_async_remote_copy(
            src_ref=total, dst_ref=red_planes.at[o - 1],
            send_sem=sum2_send.at[o], recv_sem=sum2_recv.at[o],
            device_id=(lax.rem(p + o, planes), z), device_id_type=MESH,
        )

    for o in range(1, rows):
        row_sum(o).start()
    value = part[...]
    for o in range(1, rows):
        row_sum(o).wait_recv()
        value = value + red_rows[o - 1]
    total[...] = value
    for o in range(1, planes):
        plane_sum(o).start()
    for o in range(1, planes):
        plane_sum(o).wait_recv()
        value = value + red_planes[o - 1]
    total_step = value[0:1, 0:1] / value[1:2, 0:1]

    @pl.loop(0, R // STRIP)
    def _(i):
        t = pl.multiple_of(i * STRIP, STRIP)
        strip = pl.ds(t, STRIP)
        here = d[pl.ds(t + 8, STRIP), :]
        restored[strip, :] = est[strip, :] + total_step * here
        image[strip, :] = here - total_step * image[strip, :]

    @pl.loop(1, rows)
    def _(o):
        for kind in (0, 1, 3):
            forward_copy(kind, o).wait_send()
        back_copy(1, o).wait_send()
        row_sum(o).wait_send()

    for o in range(1, planes):
        plane_sum(o).wait_send()
    for i in range(12):
        link(i, "send")


def shards(observed, estimate, spectrum):
    R, N = observed.shape[1:]
    planes, rows = lax.axis_size("planes"), lax.axis_size("rows")
    assert observed.shape[0] == 1
    L = N // rows
    high, low = cosine_parts(N)
    tile = min(256, N)
    vmem = pl.BlockSpec(memory_space=pltpu.VMEM)
    field, padded = pltpu.VMEM((R, N), F32), pltpu.VMEM((R + 16, N), F32)
    tiles = lambda *lead: pltpu.VMEM(lead + (8, 128), F32)
    dma = lambda *shape: pltpu.SemaphoreType.DMA(shape)
    restored, residual = pl.pallas_call(
        functools.partial(kernel, planes, rows),
        out_shape=(
            jax.ShapeDtypeStruct((R, N), F32),
            jax.ShapeDtypeStruct((R, N), F32),
        ),
        in_specs=[vmem] * 7,
        out_specs=(vmem,) * 2,
        scratch_shapes=[
            padded, padded, padded, padded, field, field, padded, field, field,
            pltpu.VMEM((3, R, N), F32),
            pltpu.VMEM((4, N, L), F32),
            pltpu.VMEM((2, N, L), F32),
            pltpu.VMEM((2, R, N), F32),
            pltpu.VMEM((N, L), F32),
            pltpu.VMEM((R, N), BF16), pltpu.VMEM((R, N), BF16),
            pltpu.VMEM((N, L), BF16), pltpu.VMEM((N, L), BF16),
            pltpu.VMEM((8, tile), F32), pltpu.VMEM((8, tile), F32),
            tiles(), tiles(), tiles(rows - 1), tiles(planes - 1),
            dma(7, rows), dma(7, rows), dma(12), dma(12),
            dma(rows), dma(rows), dma(planes), dma(planes),
        ],
        compiler_params=pltpu.CompilerParams(
            collective_id=0, has_side_effects=True, vmem_limit_bytes=VMEM_LIMIT
        ),
        name="deconvolve",
    )(
        observed[0], estimate[0], spectrum[0],
        jnp.asarray(high), jnp.asarray(low),
        jnp.asarray(np.ascontiguousarray(high.T)), jnp.asarray(np.ascontiguousarray(low.T)),
    )
    return (restored[None], residual[None])


def solution(mesh):
    return jax.shard_map(
        shards,
        mesh=mesh,
        in_specs=(P("planes", "rows", None), P("planes", "rows", None), P("planes", "rows", None)),
        out_specs=(P("planes", "rows", None), P("planes", "rows", None)),
        check_vma=False,
    )
```

```python
import functools
import math

import jax
import jax.numpy as jnp
import numpy as np
from jax import lax
from jax.experimental import pallas as pl
from jax.experimental.pallas import tpu as pltpu
from jax.sharding import PartitionSpec as P

HUBER_EDGE = 0.5
SMOOTHING = 0.3
MESH = pl.DeviceIdType.MESH
F32 = jnp.float32
BF16 = jnp.bfloat16
STRIP = 8
VMEM_LIMIT = 56 * 1024 * 1024


def cosine_parts(extent):
    frequency = np.arange(extent)[:, None]
    sample = np.arange(extent)[None, :]
    angles = ((2 * sample + 1) * frequency % (4 * extent)) * (math.pi / (2.0 * extent))
    norming = np.where(frequency == 0, math.sqrt(1.0 / extent), math.sqrt(2.0 / extent))
    whole = (np.cos(angles) * norming).astype(np.float32)
    high = whole.astype(jnp.bfloat16)
    low = (whole - high.astype(np.float32)).astype(jnp.bfloat16)
    return high, low


def halves(x):
    high = x.astype(BF16)
    return high, (x - high.astype(F32)).astype(BF16)


def product(ah, al, bh, bl):
    dot = functools.partial(jnp.dot, preferred_element_type=F32)
    return dot(ah, bh) + (dot(ah, bl) + dot(al, bh))


def folded(x):
    return jnp.sum(x.reshape(x.shape[0] // 8, 8, x.shape[1]), axis=0)


def kernel(
    planes, rows,
    obs, est, spec, c_hi_far, c_lo_far, t_hi_far, t_lo_far,
    restored, image,
    v, pp, pm, w, w_pm, smooth, d, d_pp, d_pm,
    sent, got, back_sent, back_got, seen, xh, xl, yh, yl,
    c_hi, c_lo, t_hi, t_lo, table_sem,
    acc_rr, acc_dot, part, total, red_rows, red_planes,
    send_sem, recv_sem, halo_send, halo_recv, sum_send, sum_recv, sum2_send, sum2_recv,
):
    p, z = lax.axis_index("planes"), lax.axis_index("rows")
    R, N = est.shape
    L = N // rows
    tile = min(256, N)
    my_row = pl.multiple_of(z * R, R)
    my_col = pl.multiple_of(z * L, L)
    has_pm, has_pp = p > 0, p < planes - 1
    has_up, has_dn = z > 0, z < rows - 1

    tables = [
        pltpu.make_async_copy(far, near, table_sem.at[i])
        for i, (far, near) in enumerate(
            ((t_hi_far, t_hi), (t_lo_far, t_lo), (c_hi_far, c_hi), (c_lo_far, c_lo))
        )
    ]
    for table in tables:
        table.start()
    v[pl.ds(8, R), :] = est[...]

    barrier = pltpu.get_barrier_semaphore()

    def greet(cond, where):
        @pl.when(cond)
        def _():
            pl.semaphore_signal(barrier, inc=1, device_id=where, device_id_type=MESH)

    for o in range(1, rows):
        pl.semaphore_signal(
            barrier, inc=1, device_id=(p, lax.rem(z + o, rows)), device_id_type=MESH
        )
    for o in range(1, planes):
        pl.semaphore_signal(
            barrier, inc=1, device_id=(lax.rem(p + o, planes), z), device_id_type=MESH
        )
    diagonals = (
        (jnp.logical_and(has_pm, has_dn), (p - 1, z + 1)),
        (jnp.logical_and(has_pp, has_up), (p + 1, z - 1)),
    )
    for cond, where in diagonals:
        greet(cond, where)
    peers = rows - 1 + planes - 1
    for cond, _ in diagonals:
        peers = peers + jnp.where(cond, 1, 0)
    pl.semaphore_wait(barrier, peers)

    def forward_copy(kind, o):
        to = lax.rem(z + o, rows)
        src = spec if kind == 0 else sent.at[kind - 1]
        return pltpu.make_async_remote_copy(
            src_ref=src.at[:, pl.ds(pl.multiple_of(to * L, L), L)],
            dst_ref=got.at[kind, pl.ds(my_row, R), :],
            send_sem=send_sem.at[kind, o],
            recv_sem=recv_sem.at[kind, o],
            device_id=(p, to),
            device_id_type=MESH,
        )

    half = R // 2

    def back_copy(kind, o, part_at):
        to = lax.rem(z + o, rows)
        length = half
        start = pl.multiple_of(to * R + part_at * half, half)
        return pltpu.make_async_remote_copy(
            src_ref=back_sent.at[kind, pl.ds(start, length), :],
            dst_ref=back_got.at[kind, pl.ds(part_at * half, length), pl.ds(my_col, L)],
            send_sem=send_sem.at[4 + 2 * kind + part_at, o],
            recv_sem=recv_sem.at[4 + 2 * kind + part_at, o],
            device_id=(p, to),
            device_id_type=MESH,
        )

    first, last = pl.ds(0, 8), pl.ds(R - 8, 8)
    body = pl.ds(8, R)
    top, low = pl.ds(8, half), pl.ds(8 + half, half)
    both = jnp.logical_and
    links = [
        (est, pm.at[body, :], (p + 1, z), has_pp, has_pm),
        (est, pp.at[body, :], (p - 1, z), has_pm, has_pp),
        (est.at[last, :], v.at[pl.ds(0, 8), :], (p, z + 1), has_dn, has_up),
        (est.at[first, :], v.at[pl.ds(R + 8, 8), :], (p, z - 1), has_up, has_dn),
        (est.at[last, :], pp.at[pl.ds(0, 8), :], (p - 1, z + 1), both(has_pm, has_dn), both(has_pp, has_up)),
        (est.at[first, :], pm.at[pl.ds(R + 8, 8), :], (p + 1, z - 1), both(has_pp, has_up), both(has_pm, has_dn)),
        (d.at[top, :], d_pm.at[pl.ds(0, half), :], (p + 1, z), has_pp, has_pm),
        (d.at[top, :], d_pp.at[pl.ds(0, half), :], (p - 1, z), has_pm, has_pp),
        (d.at[pl.ds(R, 8), :], d.at[pl.ds(0, 8), :], (p, z + 1), has_dn, has_up),
        (d.at[pl.ds(8, 8), :], d.at[pl.ds(R + 8, 8), :], (p, z - 1), has_up, has_dn),
        (d.at[low, :], d_pm.at[pl.ds(half, half), :], (p + 1, z), has_pp, has_pm),
        (d.at[low, :], d_pp.at[pl.ds(half, half), :], (p - 1, z), has_pm, has_pp),
    ]

    def link(i, act):
        src, dst, where, sends, receives = links[i]
        copy = pltpu.make_async_remote_copy(
            src_ref=src, dst_ref=dst, send_sem=halo_send.at[i], recv_sem=halo_recv.at[i],
            device_id=where, device_id_type=MESH,
        )
        @pl.when(receives if act == "recv" else sends)
        def _():
            if act == "start":
                copy.start()
            elif act == "recv":
                copy.wait_recv()
            else:
                copy.wait_send()

    for i in (2, 3, 4, 5):
        link(i, "start")
    for o in range(1, rows):
        forward_copy(0, o).start()
    for i in (0, 1):
        link(i, "start")
    got[0, pl.ds(my_row, R), :] = spec[:, pl.ds(my_col, L)]

    def columns_forward(kind, source):
        @pl.loop(0, R // 32)
        def _(i):
            strip = pl.ds(pl.multiple_of(i * 32, 32), 32)
            xh[strip, :], xl[strip, :] = halves(source[strip, :])

        @pl.loop(1, rows + 1)
        def _(o):
            at = pl.ds(pl.multiple_of(lax.rem(z + o, rows) * L, L), L)
            sent[kind - 1, :, at] = product(xh[...], xl[...], t_hi[:, at], t_lo[:, at])

            if kind != 3:
                @pl.when(o < rows)
                def _():
                    forward_copy(kind, o).start()

        got[kind, pl.ds(my_row, R), :] = sent[kind - 1, :, pl.ds(my_col, L)]

    for table in tables[:2]:
        table.wait()
    columns_forward(1, obs)
    columns_forward(2, est)

    column = lax.broadcasted_iota(jnp.int32, (STRIP, N), 1)
    strip_row = lax.broadcasted_iota(jnp.int32, (STRIP, N), 0)
    plane_at = jnp.zeros((STRIP, N), jnp.int32) + p

    def column_slope(x):
        return jnp.where(column < N - 1, pltpu.roll(x, N - 1, 1) - x, 0.0)

    def weight(x, ahead, below, plane_ok, row_at):
        slope_p = jnp.where(plane_ok, ahead - x, 0.0)
        slope_r = jnp.where(jnp.logical_and(row_at >= 0, row_at < N - 1), below - x, 0.0)
        slope_c = column_slope(x)
        size = jnp.sqrt(slope_p * slope_p + slope_r * slope_r + slope_c * slope_c)
        return 1.0 / jnp.maximum(size, HUBER_EDGE)

    for i in range(6):
        link(i, "recv")

    @pl.loop(0, R // STRIP + 1)
    def _(i):
        t = pl.multiple_of(i * STRIP, STRIP)
        block = v[pl.ds(t, STRIP + 8), :]
        w[pl.ds(t, STRIP), :] = weight(
            block[:STRIP], pp[pl.ds(t, STRIP), :], block[1 : STRIP + 1],
            plane_at < planes - 1, my_row + t - 8 + strip_row,
        )

    @pl.loop(0, R // STRIP)
    def _(i):
        t = pl.multiple_of(i * STRIP, STRIP)
        block = pm[pl.ds(t + 8, STRIP + 8), :]
        w_pm[pl.ds(t, STRIP), :] = weight(
            block[:STRIP], est[pl.ds(t, STRIP), :], block[1 : STRIP + 1],
            plane_at > 0, my_row + t + strip_row,
        )

    def regular(x, x_pm, x_pp, shift, out, begin=0, end=R, add=False):
        @pl.loop(begin // STRIP, end // STRIP)
        def _(i):
            t = pl.multiple_of(i * STRIP, STRIP)
            block = x[pl.ds(t, STRIP + 16), :]
            here = block[8 : 8 + STRIP]
            weights = w[pl.ds(t, STRIP + 8), :]
            w_here, w_up = weights[8:], weights[7 : 7 + STRIP]
            at = my_row + t + strip_row
            behind = x_pm[pl.ds(t + shift, STRIP), :]
            ahead = x_pp[pl.ds(t + shift, STRIP), :]
            in_r = jnp.where(at > 0, w_up * (here - block[7 : 7 + STRIP]), 0.0)
            out_r = jnp.where(at < N - 1, w_here * (block[9 : 9 + STRIP] - here), 0.0)
            in_p = jnp.where(plane_at > 0, w_pm[pl.ds(t, STRIP), :] * (here - behind), 0.0)
            out_p = jnp.where(plane_at < planes - 1, w_here * (ahead - here), 0.0)
            out_c = w_here * column_slope(here)
            in_c = pltpu.roll(out_c, 1, 1)
            result = SMOOTHING * ((in_p - out_p) + (in_r - out_r) + (in_c - out_c))
            out[pl.ds(t, STRIP), :] = result
            if add:
                acc_dot[...] += folded(result * here)

    regular(v, pm, pp, 8, smooth)
    columns_forward(3, smooth)

    @pl.loop(1, rows)
    def _(o):
        forward_copy(2, o).wait_send()
        forward_copy(3, o).start()

    def arrived(kind):
        @pl.loop(1, rows)
        def _(o):
            forward_copy(kind, o).wait_recv()

    def split_columns(source):
        @pl.loop(0, N // 128)
        def _(i):
            strip = pl.ds(pl.multiple_of(i * 128, 128), 128)
            yh[strip, :], yl[strip, :] = halves(source[strip, :])

    def row_forward(kind, finish):
        split_columns(got.at[kind])

        @pl.loop(0, N // tile)
        def _(i):
            at = pl.ds(pl.multiple_of(i * tile, tile), tile)
            finish(at, product(c_hi[at, :], c_lo[at, :], yh[...], yl[...]))

    def row_inverse(kind, source):
        split_columns(source)
        length = half
        for part_at in range(2):
            @pl.loop(1, rows + 1)
            def _(o):
                to = lax.rem(z + o, rows)
                at = pl.ds(pl.multiple_of(to * R + part_at * half, half), length)
                back_sent[kind, at, :] = product(t_hi[at, :], t_lo[at, :], yh[...], yl[...])

                if kind == 0:
                    @pl.when(o < rows)
                    def _():
                        back_copy(kind, o, part_at).start()

        back_got[kind, :, pl.ds(my_col, L)] = back_sent[kind, pl.ds(my_row, R), :]

    def column_inverse(kind, part_at, finish):
        @pl.loop(1, rows)
        def _(o):
            back_copy(kind, o, part_at).wait_recv()

        length = half
        here = pl.ds(part_at * half, length)

        @pl.loop(0, length // 16)
        def _(i):
            strip = pl.ds(pl.multiple_of(part_at * half + i * 16, 16), 16)
            xh[strip, :], xl[strip, :] = halves(back_got[kind, strip, :])

        @pl.loop(0, N // tile)
        def _(i):
            at = pl.ds(pl.multiple_of(i * tile, tile), tile)
            finish(at, product(xh[here, :], xl[here, :], c_hi[:, at], c_lo[:, at]))

    def keep_seen(at, spectral):
        seen[at, :] = spectral

    def keep_blurred(at, spectral):
        gain = got[0, at, :]
        seen[at, :] = gain * (seen[at, :] - gain * spectral)

    def keep_filtered(at, spectral):
        gain = got[0, at, :]
        moved = gain * (seen[at, :] - spectral)
        acc_dot[:, pl.ds(0, L)] += folded(moved * moved)
        seen[at, :] = gain * moved

    for table in tables[2:]:
        table.wait()
    acc_rr[...] = jnp.zeros_like(acc_rr)
    acc_dot[...] = jnp.zeros_like(acc_dot)
    arrived(0)
    arrived(1)
    row_forward(1, keep_seen)
    arrived(2)
    row_forward(2, keep_blurred)
    row_inverse(0, seen)
    arrived(3)
    row_forward(3, keep_filtered)
    row_inverse(1, seen)

    def keep_residual(part_at, at, x):
        here = pl.ds(part_at * half, half)
        x = x - smooth[here, at]
        d[pl.ds(8 + part_at * half, half), at] = x
        acc_rr[...] += folded(x * x)

    column_inverse(0, 0, functools.partial(keep_residual, 0))
    for i in (9, 6, 7):
        link(i, "start")

    @pl.loop(1, rows)
    def _(o):
        back_copy(0, o, 0).wait_send()
        back_copy(0, o, 1).wait_send()
        back_copy(1, o, 0).start()

    column_inverse(0, 1, functools.partial(keep_residual, 1))
    for i in (8, 10, 11):
        link(i, "start")

    @pl.loop(1, rows)
    def _(o):
        back_copy(1, o, 0).wait_send()
        back_copy(1, o, 1).start()

    for i in (6, 7, 8):
        link(i, "recv")
    regular(d, d_pm, d_pp, 0, image, 0, half, True)
    for i in (9, 10, 11):
        link(i, "recv")
    regular(d, d_pm, d_pp, 0, image, half, R, True)

    rr, dot = jnp.sum(acc_rr[...]), jnp.sum(acc_dot[...])
    which = lax.broadcasted_iota(jnp.int32, (8, 128), 0)
    part[...] = jnp.where(which == 0, rr, dot)

    def row_sum(o):
        return pltpu.make_async_remote_copy(
            src_ref=part, dst_ref=red_rows.at[o - 1],
            send_sem=sum_send.at[o], recv_sem=sum_recv.at[o],
            device_id=(p, lax.rem(z + o, rows)), device_id_type=MESH,
        )

    def plane_sum(o):
        return pltpu.make_async_remote_copy(
            src_ref=total, dst_ref=red_planes.at[o - 1],
            send_sem=sum2_send.at[o], recv_sem=sum2_recv.at[o],
            device_id=(lax.rem(p + o, planes), z), device_id_type=MESH,
        )

    for o in range(1, rows):
        row_sum(o).start()
    value = part[...]
    for o in range(1, rows):
        row_sum(o).wait_recv()
        value = value + red_rows[o - 1]
    total[...] = value
    for o in range(1, planes):
        plane_sum(o).start()
    for o in range(1, planes):
        plane_sum(o).wait_recv()
        value = value + red_planes[o - 1]
    total_step = value[0:1, 0:1] / value[1:2, 0:1]

    @pl.loop(0, R // STRIP)
    def _(i):
        t = pl.multiple_of(i * STRIP, STRIP)
        strip = pl.ds(t, STRIP)
        here = d[pl.ds(t + 8, STRIP), :]
        restored[strip, :] = est[strip, :] + total_step * here
        image[strip, :] = here - total_step * image[strip, :]

    def keep_updated(part_at, at, x):
        here = pl.ds(part_at * half, half)
        image[here, at] = image[here, at] - total_step * x

    column_inverse(1, 0, functools.partial(keep_updated, 0))
    column_inverse(1, 1, functools.partial(keep_updated, 1))

    @pl.loop(1, rows)
    def _(o):
        for kind in (0, 1, 3):
            forward_copy(kind, o).wait_send()
        back_copy(1, o, 1).wait_send()
        row_sum(o).wait_send()

    for o in range(1, planes):
        plane_sum(o).wait_send()
    for i in range(12):
        link(i, "send")


def shards(observed, estimate, spectrum):
    R, N = observed.shape[1:]
    planes, rows = lax.axis_size("planes"), lax.axis_size("rows")
    assert observed.shape[0] == 1
    L = N // rows
    high, low = cosine_parts(N)
    tile = min(256, N)
    vmem = pl.BlockSpec(memory_space=pltpu.VMEM)
    field, padded = pltpu.VMEM((R, N), F32), pltpu.VMEM((R + 16, N), F32)
    tiles = lambda *lead: pltpu.VMEM(lead + (8, 128), F32)
    dma = lambda *shape: pltpu.SemaphoreType.DMA(shape)
    restored, residual = pl.pallas_call(
        functools.partial(kernel, planes, rows),
        out_shape=(
            jax.ShapeDtypeStruct((R, N), F32),
            jax.ShapeDtypeStruct((R, N), F32),
        ),
        in_specs=[vmem] * 3 + [pl.BlockSpec(memory_space=pl.ANY)] * 4,
        out_specs=(vmem,) * 2,
        scratch_shapes=[
            padded, padded, padded, padded, field, field, padded, field, field,
            pltpu.VMEM((3, R, N), F32),
            pltpu.VMEM((4, N, L), F32),
            pltpu.VMEM((2, N, L), F32),
            pltpu.VMEM((2, R, N), F32),
            pltpu.VMEM((N, L), F32),
            pltpu.VMEM((R, N), BF16), pltpu.VMEM((R, N), BF16),
            pltpu.VMEM((N, L), BF16), pltpu.VMEM((N, L), BF16),
            *[pltpu.VMEM((N, N), BF16)] * 4, dma(4),
            pltpu.VMEM((8, tile), F32), pltpu.VMEM((8, N), F32),
            tiles(), tiles(), tiles(rows - 1), tiles(planes - 1),
            dma(8, rows), dma(8, rows), dma(12), dma(12),
            dma(rows), dma(rows), dma(planes), dma(planes),
        ],
        compiler_params=pltpu.CompilerParams(
            collective_id=0, has_side_effects=True, vmem_limit_bytes=VMEM_LIMIT
        ),
        name="deconvolve",
    )(
        observed[0], estimate[0], spectrum[0],
        jnp.asarray(high), jnp.asarray(low),
        jnp.asarray(np.ascontiguousarray(high.T)), jnp.asarray(np.ascontiguousarray(low.T)),
    )
    return (restored[None], residual[None])


def solution(mesh):
    return jax.shard_map(
        shards,
        mesh=mesh,
        in_specs=(P("planes", "rows", None), P("planes", "rows", None), P("planes", "rows", None)),
        out_specs=(P("planes", "rows", None), P("planes", "rows", None)),
        check_vma=False,
    )
```
